256 devices in a mesh: surf: 16 (over y, x), hist: 16 (over z, core).
Axes of the slice: x: 4, y: 4, z: 8, core: 2. Of those that a mesh axis runs over, the one named last changes fastest.
Arguments:
- excitation: float32 [2, 64, 8192], P(None, None, 'surf'), may hold values from -6 to 6
- history: bfloat16 [128, 64, 8192], P('hist', None, 'surf'), may hold values from -6 to 6
- blocks: bfloat16 [128, 64, 8, 128, 128], P('hist', 'surf'), may hold values from -0.015625 to 0.015625
- pattern: int32 [128, 64, 8], P('hist', 'surf'), may hold values from 0 to 63, as said below
- near_inverse: float32 [64, 128, 128], P('surf')
Outputs:
- currents: float32 [2, 64, 8192], P(None, None, 'surf')
The draws below stay inside these ranges and needn't reach their ends.
Inputs may be any that keep to these rules, and one draw needn't show every extreme that they name: `pattern`: slot 0 of every history step and row block names that row block itself; every other slot names a column block drawn independently and evenly for each history step, row block and slot.
All inputs are finite; a program needn't handle non-finite values.
Results may differ from the reference program's by a relative error of at most 0.0003.
Values may be sent and summed in bfloat16 or wider, within the bound.
No kernel may reach another device: no remote copies, remote signals or barrier semaphores. Data moves between devices by JAX's collectives and lax.ppermute only.
A program may use at most 128 MiB of HBM per device.

```python
import jax
import jax.numpy as jnp
from jax import lax

BS = 128
S = 8
R = 64
NB = 64
P_SIZE = 8192
K = 128


def draw_pattern(key, part):
    key = jax.random.fold_in(key, 1)
    own_rows = jnp.broadcast_to(jnp.arange(NB, dtype=jnp.int32)[None, :, None], (K, NB, 1))
    others = jax.random.randint(key, (K, NB, S - 1), 0, NB, dtype=jnp.int32)
    return jnp.concatenate([own_rows, others], axis=2).astype(jnp.int32)


def draw_near_inverse(key, part):
    key = jax.random.fold_in(key, 2)
    key_main, key_scale = jax.random.split(key)
    noise = jax.random.normal(key_main, (NB, BS, BS), jnp.float32) * (0.4 / BS ** 0.5)
    scales = jax.random.uniform(key_scale, (NB, BS, 1), jnp.float32, 0.5, 1.5)
    return (jnp.eye(BS, dtype=jnp.float32)[None] + noise) * scales


def shard_levels(rng, shape, shards, low, high):
    gain = 1.0
    for position, blocks in shards:
        heights = jax.random.uniform(jax.random.fold_in(jax.random.fold_in(rng, 6), position), (blocks,), jnp.float32, low / len(shards), high / len(shards))
        gain = gain * jnp.repeat(jnp.exp(heights), shape[position] // blocks).reshape((-1,) + (1,) * (len(shape) - 1 - position))
    return gain


def bell_draw(own_key, extent, scale, reach, shards=(), kind=jnp.bfloat16):
    loudness = shard_levels(own_key, extent, shards, -0.22, 0.18) if shards else 1.0
    drawn = jax.random.normal(own_key, extent, jnp.float32) * scale * loudness
    return jnp.minimum(jnp.maximum(drawn, -reach), reach).astype(kind)


def setup_inputs(seed: int = 0) -> dict:
    key_of = jax.random.split(jax.random.key(seed), 6)
    excitation = bell_draw(key_of[0], (2, R, P_SIZE), 1.0, 6.0, ((2, 16),), jnp.float32)
    history = bell_draw(key_of[1], (K, R, P_SIZE), 1.0, 6.0, ((0, 16), (2, 16)))
    blocks = bell_draw(key_of[2], (K, NB, S, BS, BS), (BS * S * K) ** -0.5, 0.015625, ((0, 16), (1, 16)))
    pattern = draw_pattern(jax.random.fold_in(key_of[5], 71), 0)
    near_inverse = draw_near_inverse(jax.random.fold_in(key_of[5], 71), 0)
    return {"excitation": excitation, "history": history, "blocks": blocks, "pattern": pattern, "near_inverse": near_inverse}


def retarded(blocks, pattern, hist):
    hist_blocks = hist.reshape(K, R, NB, BS)

    def one_step(total, inputs):
        blk, cols, slab = inputs
        picked = slab[:, cols]
        term = jnp.einsum("isab,risb->ria", blk.astype(jnp.float32), picked.astype(jnp.float32))
        return total + term, None

    start = jnp.zeros((R, NB, BS), jnp.float32)
    total, unused = lax.scan(one_step, start, (blocks, pattern, hist_blocks))
    return total.reshape(R, P_SIZE)


def near_solve(near_inverse, field):
    out = jnp.einsum("iab,rib->ria", near_inverse, field.reshape(R, NB, BS), precision=lax.Precision.HIGHEST)
    return out.reshape(R, P_SIZE)


def reference(excitation, history, blocks, pattern, near_inverse):
    field_one = excitation[0] - retarded(blocks, pattern, history)
    first = near_solve(near_inverse, field_one)
    history_two = jnp.concatenate([first.astype(jnp.bfloat16)[None], history[:-1]], axis=0)
    field_two = excitation[1] - retarded(blocks, pattern, history_two)
    second = near_solve(near_inverse, field_two)
    return jnp.stack([first, second])
```

```python
import jax
import jax.numpy as jnp
from jax import lax
from jax.experimental import pallas as pl
from jax.experimental.pallas import tpu as pltpu
from jax.sharding import Mesh
from jax.sharding import PartitionSpec as P

F32 = jnp.float32
BF16 = jnp.bfloat16
Y, X, Z, C = 4, 4, 8, 2
STEPS, ROWS, SLOTS, BS = 8, 4, 8, 128
CH = 64
CHZ = CH // Z
HALF = STEPS // 2
NT = (((1,), (1,)), ((), ()))
VMEM_LIMIT = 56 * 1024 * 1024


def turn(array, axis, by):
    length = lax.axis_size(axis)
    return lax.ppermute(array, axis, [(i, (i + by) % length) for i in range(length)])


def swap_cores(array):
    return lax.ppermute(array, "core", [(0, 1), (1, 0)])


def ring(array, axis):
    half = array.shape[0] // 2
    below = turn(array, axis, 1)
    above = turn(array, axis, -1)
    far_low = turn(below[:half], axis, 1)
    far_high = turn(above[half:], axis, -1)
    return jnp.concatenate([array, below, above, far_low, far_high], axis=0)


def gather_history(history):
    first, second = history[:HALF], history[HALF:]
    return jnp.concatenate([ring(ring(first, "x"), "y"), ring(ring(second, "y"), "x")], axis=0)


def entries(cols, steps):
    place = jnp.array([0, 1, 3, 2], jnp.int32)
    dy = place[(lax.axis_index("y") - cols // (X * ROWS)) % Y]
    dx = place[(lax.axis_index("x") - (cols // ROWS) % X) % X]
    early = (dy * X + dx) * HALF + steps
    late = Y * X * HALF + (dx * Y + dy) * HALF + steps - HALF
    return jnp.where(steps < HALF, early, late) * ROWS + cols % ROWS


def field_kernel(now_idx, past_idx, blocks_ref, next_ref, table_ref, out_ref, acc):
    k = pl.program_id(0)

    def slab(code):
        lane = pl.multiple_of(lax.rem(code, ROWS) * BS, BS)
        return table_ref[lax.div(code, ROWS), :, pl.ds(lane, BS)]

    def gathered(idx, row):
        base = (k * ROWS + row) * SLOTS
        return jnp.concatenate([slab(idx[base + s]) for s in range(SLOTS)], axis=1)

    def matrix(ref, lead, row):
        return jnp.concatenate([ref[lead + (row, s)] for s in range(SLOTS)], axis=1)

    @pl.when(k == 0)
    def _():
        for row in range(ROWS):
            first = lax.dot_general(gathered(now_idx, row), matrix(blocks_ref, (0,), row), NT, preferred_element_type=F32)
            last = []
            for s in range(SLOTS):
                last.append(slab(past_idx[row * SLOTS + s]))
            second = lax.dot_general(jnp.concatenate(last, axis=1), matrix(next_ref, (), row), NT, preferred_element_type=F32)
            acc[row, :CH] = first
            acc[row, CH:] = second

    @pl.when(k > 0)
    def _():
        for row in range(ROWS):
            both = jnp.concatenate([gathered(now_idx, row), gathered(past_idx, row)], axis=0)
            acc[row] += lax.dot_general(both, matrix(blocks_ref, (0,), row), NT, preferred_element_type=F32)

    @pl.when(k == STEPS - 1)
    def _():
        for row in range(ROWS):
            for f in range(2):
                for z in range(Z):
                    start = f * CH + z * CHZ
                    out_ref[row // 2, z, row % 2, f] = acc[row, start : start + CHZ]


def field_partials(blocks, following, table, now_idx, past_idx):
    return pl.pallas_call(
        field_kernel,
        grid_spec=pltpu.PrefetchScalarGridSpec(
            num_scalar_prefetch=2,
            grid=(STEPS,),
            in_specs=[
                pl.BlockSpec((1, ROWS, SLOTS, BS, BS), lambda k, a, b: (k, 0, 0, 0, 0)),
                pl.BlockSpec(memory_space=pltpu.VMEM),
                pl.BlockSpec(memory_space=pltpu.VMEM),
            ],
            out_specs=pl.BlockSpec(memory_space=pltpu.VMEM),
            scratch_shapes=[pltpu.VMEM((ROWS, 2 * CH, BS), F32)],
        ),
        out_shape=jax.ShapeDtypeStruct((2, Z, 2, 2, CHZ, BS), F32),
        compiler_params=pltpu.CompilerParams(vmem_limit_bytes=VMEM_LIMIT),
        name="retarded_partials",
    )(now_idx, past_idx, blocks, following, table)


def exact_dot(a, b):
    return lax.dot_general(a, b, NT, precision=lax.Precision.HIGHEST, preferred_element_type=F32)


def first_kernel(parts_ref, excite_ref, near_ref, current_ref, low_ref, rest_ref):
    total = parts_ref[0]
    for z in range(1, Z):
        total = total + parts_ref[z]
    solved = []
    for row in range(2):
        at = row * 2 * CHZ
        field = excite_ref[0, row] - total[at : at + CHZ]
        solved.append(exact_dot(field, near_ref[row]))
        rest_ref[row] = excite_ref[1, row] - total[at + CHZ : at + 2 * CHZ]
    both = jnp.concatenate(solved, axis=0)
    current_ref[...] = both
    low = both.astype(BF16)
    for s in range(Y * X):
        low_ref[s] = low


def first_solve(parts, excite, near):
    return pl.pallas_call(
        first_kernel,
        out_shape=(
            jax.ShapeDtypeStruct((2 * CHZ, BS), F32),
            jax.ShapeDtypeStruct((Y * X, 2 * CHZ, BS), BF16),
            jax.ShapeDtypeStruct((2, CHZ, BS), F32),
        ),
        name="first_solve",
    )(parts, excite, near)


def second_kernel(idx, mine_ref, other_ref, blocks_ref, rest_ref, near_ref, current_ref, out_ref, table):
    for h, ref in enumerate((mine_ref, other_ref)):
        for s in range(Y * X):
            wide = ref[s].astype(F32)
            for row in range(2):
                table[(h * Y * X + s) * 2 + row] = wide[row * CHZ : (row + 1) * CHZ]
    solved = []
    for row in range(2):
        picked = [table[idx[row * SLOTS + s]].astype(BF16) for s in range(SLOTS)]
        matrix = jnp.concatenate([blocks_ref[(row * SLOTS + s) * BS : (row * SLOTS + s + 1) * BS] for s in range(SLOTS)], axis=1)
        term = lax.dot_general(jnp.concatenate(picked, axis=1), matrix, NT, preferred_element_type=F32)
        solved.append(exact_dot(rest_ref[row] - term, near_ref[row]))
    second = jnp.concatenate(solved, axis=0)
    first = current_ref[...]
    for z in range(Z):
        out_ref[z, 0] = first
        out_ref[z, 1] = second


def second_solve(idx, mine, other, blocks, rest, near, current):
    return pl.pallas_call(
        second_kernel,
        in_specs=[pl.BlockSpec(memory_space=pltpu.SMEM)] + [pl.BlockSpec(memory_space=pltpu.VMEM)] * 6,
        out_specs=pl.BlockSpec(memory_space=pltpu.VMEM),
        out_shape=jax.ShapeDtypeStruct((Z, 2, 2 * CHZ, BS), F32),
        scratch_shapes=[pltpu.VMEM((2 * Y * X * 2, CHZ, BS), F32)],
        name="second_solve",
    )(idx, mine, other, blocks, rest, near, current)


def spread_front(blocks, pattern):
    core, z = lax.axis_index("core"), lax.axis_index("z")
    size = 2 * SLOTS * BS
    codes = jnp.broadcast_to(pattern[0].astype(BF16).reshape(2, 1, 2 * SLOTS), (2, 16, 2 * SLOTS))
    codes = jnp.pad(codes, ((0, 0), (0, 0), (0, BS - 2 * SLOTS)))
    packs = jnp.concatenate([blocks[0].reshape(2, size, BS), codes], axis=1)
    sent = lax.ppermute(packs[1], "core", [(0, 1)])
    held = jnp.where(core == 0, packs[0], sent)
    held = jnp.where(z % 8 == 4, lax.ppermute(held, "z", [(0, 4)]), held)
    held = jnp.where(z % 4 == 2, lax.ppermute(held, "z", [(0, 2), (4, 6)]), held)
    held = jnp.where(z % 2 == 1, lax.ppermute(held, "z", [(0, 1), (2, 3), (4, 5), (6, 7)]), held)
    return held, held[size, : 2 * SLOTS].astype(jnp.int32)


def local(excitation, history, blocks, pattern, near_inverse):
    core, z = lax.axis_index("core"), lax.axis_index("z")
    bands = lax.axis_size(("z", "core"))
    back = [(i + 1, i) for i in range(bands - 1)]
    following = lax.ppermute(blocks[0], ("z", "core"), back)
    following_pattern = lax.ppermute(pattern[0], ("z", "core"), back)
    table = gather_history(history)
    front, front_pattern = spread_front(blocks, pattern)

    steps = jnp.arange(STEPS, dtype=jnp.int32)[:, None, None]
    now_idx = entries(pattern, steps)
    past_idx = jnp.concatenate(
        [entries(following_pattern, jnp.int32(STEPS - 1))[None], entries(pattern, steps - 1)[1:]], axis=0
    )
    partial = field_partials(blocks, following, table, now_idx.reshape(-1), past_idx.reshape(-1))

    kept = lax.dynamic_index_in_dim(partial, core, 0, keepdims=False)
    given = lax.dynamic_index_in_dim(partial, 1 - core, 0, keepdims=False)
    pair = (kept + swap_cores(given)).reshape(Z, 4 * CHZ, BS)
    parts = lax.all_to_all(pair, "z", 0, 0)

    excite = lax.dynamic_slice(excitation, (0, z * CHZ, core * 2 * BS), (2, CHZ, 2 * BS))
    excite = excite.reshape(2, CHZ, 2, BS).transpose(0, 2, 1, 3)
    near = lax.dynamic_slice(near_inverse, (core * 2, 0, 0), (2, BS, BS))
    current, low, rest = first_solve(parts, excite, near)

    mine = lax.all_to_all(low, ("y", "x"), 0, 0)
    other = swap_cores(mine)
    block_core = (front_pattern % ROWS) // 2
    front_idx = ((block_core ^ core) * Y * X + front_pattern // ROWS) * 2 + front_pattern % 2
    ready = second_solve(front_idx, mine, other, front, rest, near, current)

    kept = lax.all_to_all(ready, "z", 0, 0)
    given = swap_cores(kept)
    both = jnp.stack([jnp.where(core == 0, kept, given), jnp.where(core == 0, given, kept)])
    both = both.reshape(C, Z, 2, 2, CHZ, BS)
    return both.transpose(2, 1, 4, 0, 3, 5).reshape(2, CH, ROWS * BS)


def solution(mesh):
    split = Mesh(mesh.devices.reshape(Y, X, Z, C), ("y", "x", "z", "core"))
    surf, hist = ("y", "x"), ("z", "core")
    in_specs = (
        P(None, None, surf),
        P(hist, None, surf),
        P(hist, surf, None, None, None),
        P(hist, surf, None),
        P(surf, None, None),
    )
    out_specs = P(None, None, surf)
    return jax.shard_map(local, mesh=split, in_specs=in_specs, out_specs=out_specs, check_vma=False)
```

```python
import jax
import jax.numpy as jnp
from jax import lax
from jax.experimental import pallas as pl
from jax.experimental.pallas import tpu as pltpu
from jax.sharding import Mesh
from jax.sharding import PartitionSpec as P

F32 = jnp.float32
BF16 = jnp.bfloat16
Y, X, Z, C = 4, 4, 8, 2
STEPS, ROWS, SLOTS, BS = 8, 4, 8, 128
CH = 64
CHZ = CH // Z
SIDE = 2 * SLOTS * BS
PAIR = SIDE + 16
NT = (((1,), (1,)), ((), ()))
VMEM_LIMIT = 48 * 1024 * 1024
PACK_LIMIT = 58 * 1024 * 1024
SMALL_LIMIT = 4 * 1024 * 1024


def swap_cores(array):
    return lax.ppermute(array, "core", [(0, 1), (1, 0)])


def hop_pairs(phase, by):
    pairs = []
    for y in range(Y):
        for x in range(X):
            for z in range(Z):
                for core in range(C):
                    if core == phase:
                        to = (y, (x + by) % X)
                    else:
                        to = ((y + by) % Y, x)
                    pairs.append((((y * X + x) * Z + z) * C + core, ((to[0] * X + to[1]) * Z + z) * C + core))
    return pairs


def hop(array, phase, by):
    return lax.ppermute(array, ("y", "x", "z", "core"), hop_pairs(phase, by))


def near_hops(array, phase):
    return hop(array, phase, 1), hop(array, phase, -1)


def first_axis(history):
    below, above = near_hops(history, 0)
    half = STEPS // 2
    far = hop(below[:half], 0, 1), hop(above[half:], 0, -1)
    return jnp.concatenate([history, below]), jnp.concatenate([above, *far])


def entries(cols, steps):
    dy = (lax.axis_index("y") - cols // (X * ROWS)) % Y
    dx = (lax.axis_index("x") - (cols // ROWS) % X) % X
    dy, dx = dy ^ (dy >> 1), dx ^ (dx >> 1)
    slot = jnp.where(lax.axis_index("core") == 0, dy * X + dx, dx * Y + dy)
    return (slot * STEPS + steps) * ROWS + cols % ROWS


def pack_kernel(blocks_ref, pattern_ref, out_ref, codes, sems):
    copies = []
    for pair in range(2):
        for part in range(4):
            size = SIDE // 4
            source = blocks_ref.at[pl.ds(pair * SIDE + part * size, size)]
            target = out_ref.at[pair, pl.ds(part * size, size)]
            copies.append(pltpu.make_async_copy(source, target, sems.at[len(copies)]))
    for copy in copies:
        copy.start()
    codes[...] = jnp.zeros_like(codes)
    codes[:ROWS, :SLOTS] = pattern_ref[0].astype(F32)
    for pair in range(2):
        out_ref[pair, SIDE:] = codes[...].astype(BF16)
    for copy in copies:
        copy.wait()


def packed_front(blocks, pattern):
    return pl.pallas_call(
        pack_kernel,
        in_specs=[pl.BlockSpec(memory_space=pltpu.HBM), pl.BlockSpec(memory_space=pltpu.VMEM)],
        out_specs=pl.BlockSpec(memory_space=pltpu.VMEM),
        out_shape=jax.ShapeDtypeStruct((2, PAIR, BS), BF16),
        scratch_shapes=[pltpu.VMEM((16, BS), F32), pltpu.SemaphoreType.DMA((8,))],
        compiler_params=pltpu.CompilerParams(vmem_limit_bytes=PACK_LIMIT),
        name="packed_front",
    )(blocks.reshape(-1, BS), pattern)


def packed_codes(pack):
    return pack[SIDE : SIDE + ROWS, :SLOTS].astype(jnp.int32)


def picked_rows(table_ref, idx, base):
    parts = []
    for s in range(SLOTS):
        code = idx[base + s]
        lane = pl.multiple_of(lax.rem(code, ROWS) * BS, BS)
        parts.append(table_ref[lax.div(code, ROWS), :, pl.ds(lane, BS)])
    return jnp.concatenate(parts, axis=1)


def slot_product(rows, squares):
    return lax.dot_general(rows, jnp.concatenate(squares, axis=1), NT, preferred_element_type=F32)


def field_kernel(now_idx, past_idx, is_last, blocks_ref, next_ref, *refs):
    parts, (out_ref, acc, squares, table, sems) = refs[:PARTS], refs[PARTS:]
    size = parts[0].shape[0]
    tables = [
        pltpu.make_async_copy(part, table.at[pl.ds(i * size, size)], sems.at[STEPS + i]) for i, part in enumerate(parts)
    ]
    arriving = [pltpu.make_async_copy(blocks_ref.at[k], squares.at[k], sems.at[k]) for k in range(STEPS)]
    for copy in tables + arriving:
        copy.start()
    for copy in tables:
        copy.wait()
    for row in range(ROWS):
        last = picked_rows(table, past_idx, row * SLOTS)
        at = (row % 2) * SLOTS
        matrix = [next_ref[row // 2, (at + s) * BS : (at + s + 1) * BS] for s in range(SLOTS)]
        acc[row, CH:] = jnp.where(is_last[0] == 1, 0.0, slot_product(last, matrix))
    for k in range(STEPS):
        arriving[k].wait()
        for row in range(ROWS):
            base = (k * ROWS + row) * SLOTS
            matrix = [squares[k, row, s] for s in range(SLOTS)]
            now = picked_rows(table, now_idx, base)
            if k == 0:
                acc[row, :CH] = slot_product(now, matrix)
            else:
                past = picked_rows(table, past_idx, base)
                acc[row] += slot_product(jnp.concatenate([now, past]), matrix)
    for row in range(ROWS):
        for f in range(2):
            for z in range(Z):
                start = f * CH + z * CHZ
                out_ref[z, row // 2, row % 2, f] = acc[row, start : start + CHZ]


IN_SMEM = pl.BlockSpec(memory_space=pltpu.SMEM)
IN_VMEM = pl.BlockSpec(memory_space=pltpu.VMEM)
IN_HBM = pl.BlockSpec(memory_space=pltpu.HBM)
ANYWHERE = pl.BlockSpec(memory_space=pl.ANY)
SLAB = (CH, ROWS * BS)
PARTS = 8


def field_partials(blocks, following, parts, now_idx, past_idx, is_last):
    return pl.pallas_call(
        field_kernel,
        in_specs=[IN_SMEM] * 3 + [IN_HBM, IN_VMEM] + [ANYWHERE] * PARTS,
        out_specs=IN_VMEM,
        out_shape=jax.ShapeDtypeStruct((Z, C, 2, 2, CHZ, BS), F32),
        scratch_shapes=[
            pltpu.VMEM((ROWS, 2 * CH, BS), F32),
            pltpu.VMEM((STEPS, ROWS, SLOTS, BS, BS), BF16),
            pltpu.VMEM((Y * X * STEPS, *SLAB), BF16),
            pltpu.SemaphoreType.DMA((STEPS + PARTS,)),
        ],
        compiler_params=pltpu.CompilerParams(vmem_limit_bytes=VMEM_LIMIT),
        cost_estimate=pl.CostEstimate(flops=1 << 30, bytes_accessed=1 << 24, transcendentals=0),
        name="field_partials",
    )(now_idx, past_idx, is_last, blocks, following, *parts)


def exact_dot(a, b):
    return lax.dot_general(a, b, NT, precision=lax.Precision.HIGHEST, preferred_element_type=F32)


def first_kernel(parts_ref, excite_ref, near_ref, current_ref, low_ref, rest_ref):
    total = parts_ref[0]
    for band in range(1, Z * C):
        total = total + parts_ref[band]
    solved = []
    for row in range(2):
        at = row * 2 * CHZ
        field = excite_ref[0, row] - total[at : at + CHZ]
        solved.append(exact_dot(field, near_ref[row]))
        rest_ref[row] = excite_ref[1, row] - total[at + CHZ : at + 2 * CHZ]
    both = jnp.concatenate(solved, axis=0)
    current_ref[...] = both
    low = both.astype(BF16)
    for s in range(Y * X):
        low_ref[s] = low


def first_solve(parts, excite, near):
    return pl.pallas_call(
        first_kernel,
        out_shape=(
            jax.ShapeDtypeStruct((2 * CHZ, BS), F32),
            jax.ShapeDtypeStruct((Y * X, 2 * CHZ, BS), BF16),
            jax.ShapeDtypeStruct((2, CHZ, BS), F32),
        ),
        compiler_params=pltpu.CompilerParams(vmem_limit_bytes=SMALL_LIMIT),
        name="first_solve",
    )(parts, excite, near)


def second_kernel(idx, mine_ref, other_ref, blocks_ref, rest_ref, near_ref, current_ref, out_ref, table):
    for h, ref in enumerate((mine_ref, other_ref)):
        for s in range(Y * X):
            wide = ref[s].astype(F32)
            for row in range(2):
                table[(h * Y * X + s) * 2 + row] = wide[row * CHZ : (row + 1) * CHZ]
    solved = []
    for row in range(2):
        picked = [table[idx[row * SLOTS + s]].astype(BF16) for s in range(SLOTS)]
        matrix = jnp.concatenate([blocks_ref[(row * SLOTS + s) * BS : (row * SLOTS + s + 1) * BS] for s in range(SLOTS)], axis=1)
        term = lax.dot_general(jnp.concatenate(picked, axis=1), matrix, NT, preferred_element_type=F32)
        solved.append(exact_dot(rest_ref[row] - term, near_ref[row]))
    second = jnp.concatenate(solved, axis=0)
    first = current_ref[...]
    for z in range(Z):
        out_ref[z, 0] = first
        out_ref[z, 1] = second


def second_solve(idx, mine, other, blocks, rest, near, current):
    return pl.pallas_call(
        second_kernel,
        in_specs=[pl.BlockSpec(memory_space=pltpu.SMEM)] + [pl.BlockSpec(memory_space=pltpu.VMEM)] * 6,
        out_specs=pl.BlockSpec(memory_space=pltpu.VMEM),
        out_shape=jax.ShapeDtypeStruct((Z, 2, 2 * CHZ, BS), F32),
        scratch_shapes=[pltpu.VMEM((2 * Y * X * 2, CHZ, BS), F32)],
        compiler_params=pltpu.CompilerParams(vmem_limit_bytes=SMALL_LIMIT),
        name="second_solve",
    )(idx, mine, other, blocks, rest, near, current)


SPREAD = (((0, 2), (7, 5)), ((0, 1), (2, 3), (5, 4), (7, 6)))


def spread(array, step, tie):
    z = lax.axis_index("z")
    received = lax.ppermute(tie(array), "z", SPREAD[step])
    hit = z == SPREAD[step][0][1]
    for _, target in SPREAD[step][1:]:
        hit = hit | (z == target)
    return jnp.where(hit, received, array)


def after(array, *events):
    return lax.optimization_barrier((array, *events))[0]


def local(excitation, history, blocks, pattern, near_inverse):
    core, z = lax.axis_index("core"), lax.axis_index("z")
    bands = lax.axis_size(("z", "core"))

    line = first_axis(history)
    pack = packed_front(blocks, pattern)
    below = hop(line[0], 1, 1)
    above = hop(line[1], 1, -1)
    below_rest = hop(line[1], 1, 1)
    above_rest = hop(line[0], 1, -1)
    far = hop(below, 1, 1), hop(above, 1, -1)
    following = lax.ppermute(pack, ("z", "core"), [(i, (i - 1) % bands) for i in range(bands)])
    given = jnp.where(core == 0, pack[1], following[0])
    front = jnp.where(z == 0, pack[0], following[1])
    front = jnp.where(core == (z == 0), swap_cores(given), front)
    front = spread(front, 0, lambda new: after(new, below_rest, above_rest))

    pattern = after(pattern, line)
    steps = jnp.arange(STEPS, dtype=jnp.int32)[:, None, None]
    now_idx = entries(pattern, steps)
    past_cols = jnp.concatenate([packed_codes(following[0])[None], pattern[1:]])
    past_idx = entries(past_cols, (steps - 1) % STEPS)
    parts = (*line, below, below_rest, above_rest, above, *far)
    is_last = (z * C + core == bands - 1).astype(jnp.int32).reshape(1)
    partial = field_partials(blocks, following, parts, now_idx.reshape(-1), past_idx.reshape(-1), is_last)
    parts = lax.all_to_all(partial.reshape(Z * C, 4 * CHZ, BS), ("z", "core"), 0, 0)

    excite = lax.dynamic_slice(excitation, (0, z * CHZ, core * 2 * BS), (2, CHZ, 2 * BS))
    excite = excite.reshape(2, CHZ, 2, BS).transpose(0, 2, 1, 3)
    near = lax.dynamic_slice(near_inverse, (core * 2, 0, 0), (2, BS, BS))
    current, low, rest = first_solve(parts, excite, near)
    front = spread(front, 1, lambda new: after(new, current))

    mine = lax.all_to_all(low, ("y", "x"), 0, 0)
    other = swap_cores(mine)
    front_cols = lax.dynamic_slice_in_dim(packed_codes(front), core * 2, 2).reshape(-1)
    front_idx = (((front_cols % ROWS) // 2 ^ core) * Y * X + front_cols // ROWS) * 2 + front_cols % 2
    ready = second_solve(front_idx, mine, other, front, rest, near, current)

    kept = lax.all_to_all(ready, "z", 0, 0)
    given = swap_cores(kept)
    both = jnp.stack([jnp.where(core == 0, kept, given), jnp.where(core == 0, given, kept)])
    both = both.reshape(C, Z, 2, 2, CHZ, BS)
    return both.transpose(2, 1, 4, 0, 3, 5).reshape(2, CH, ROWS * BS)


def solution(mesh):
    split = Mesh(mesh.devices.reshape(Y, X, Z, C), ("y", "x", "z", "core"))
    surf, hist = ("y", "x"), ("z", "core")
    in_specs = (
        P(None, None, surf),
        P(hist, None, surf),
        P(hist, surf, None, None, None),
        P(hist, surf, None),
        P(surf, None, None),
    )
    out_specs = P(None, None, surf)
    return jax.shard_map(local, mesh=split, in_specs=in_specs, out_specs=out_specs, check_vma=False)
```

```python
import jax
import jax.numpy as jnp
from jax import lax
from jax.experimental import pallas as pl
from jax.experimental.pallas import tpu as pltpu
from jax.sharding import Mesh
from jax.sharding import PartitionSpec as P

F32 = jnp.float32
BF16 = jnp.bfloat16
Y, X, Z, C = 4, 4, 8, 2
STEPS, ROWS, SLOTS, BS = 8, 4, 8, 128
CH = 64
CHZ = CH // Z
SIDE = 2 * SLOTS * BS
PAIR = SIDE + 16
NT = (((1,), (1,)), ((), ()))
VMEM_LIMIT = 22 * 1024 * 1024
PACK_LIMIT = 58 * 1024 * 1024
SMALL_LIMIT = 4 * 1024 * 1024


def swap_cores(array):
    return lax.ppermute(array, "core", [(0, 1), (1, 0)])


def hop_pairs(phase, by):
    pairs = []
    for y in range(Y):
        for x in range(X):
            for z in range(Z):
                for core in range(C):
                    if core == phase:
                        to = (y, (x + by) % X)
                    else:
                        to = ((y + by) % Y, x)
                    pairs.append((((y * X + x) * Z + z) * C + core, ((to[0] * X + to[1]) * Z + z) * C + core))
    return pairs


def hop(array, phase, by):
    return lax.ppermute(array, ("y", "x", "z", "core"), hop_pairs(phase, by))


def near_hops(array, phase):
    return hop(array, phase, 1), hop(array, phase, -1)


def first_axis(history):
    below, above = near_hops(history, 0)
    half = STEPS // 2
    far = hop(below[:half], 0, 1), hop(above[half:], 0, -1)
    return jnp.concatenate([history, below]), jnp.concatenate([above, *far])


def entries(cols, steps):
    dy = (lax.axis_index("y") - cols // (X * ROWS)) % Y
    dx = (lax.axis_index("x") - (cols // ROWS) % X) % X
    dy, dx = dy ^ (dy >> 1), dx ^ (dx >> 1)
    slot = jnp.where(lax.axis_index("core") == 0, dy * X + dx, dx * Y + dy)
    return (slot * STEPS + steps) * ROWS + cols % ROWS


def pack_kernel(blocks_ref, pattern_ref, out_ref, codes, sems):
    copies = []
    for pair in range(2):
        for part in range(4):
            size = SIDE // 4
            source = blocks_ref.at[pl.ds(pair * SIDE + part * size, size)]
            target = out_ref.at[pair, pl.ds(part * size, size)]
            copies.append(pltpu.make_async_copy(source, target, sems.at[len(copies)]))
    for copy in copies:
        copy.start()
    codes[...] = jnp.zeros_like(codes)
    codes[:ROWS, :SLOTS] = pattern_ref[0].astype(F32)
    for pair in range(2):
        out_ref[pair, SIDE:] = codes[...].astype(BF16)
    for copy in copies:
        copy.wait()


def packed_front(blocks, pattern):
    return pl.pallas_call(
        pack_kernel,
        in_specs=[pl.BlockSpec(memory_space=pltpu.HBM), pl.BlockSpec(memory_space=pltpu.VMEM)],
        out_specs=pl.BlockSpec(memory_space=pltpu.VMEM),
        out_shape=jax.ShapeDtypeStruct((2, PAIR, BS), BF16),
        scratch_shapes=[pltpu.VMEM((16, BS), F32), pltpu.SemaphoreType.DMA((8,))],
        compiler_params=pltpu.CompilerParams(vmem_limit_bytes=PACK_LIMIT),
        name="packed_front",
    )(blocks.reshape(-1, BS), pattern)


def packed_codes(pack):
    return pack[SIDE : SIDE + ROWS, :SLOTS].astype(jnp.int32)


def picked_rows(table, last, idx, base):
    parts = []
    for s in range(SLOTS):
        code = idx[base + s]
        lane = pl.multiple_of(lax.rem(code, ROWS) * BS, BS)
        slab = lax.div(code, ROWS)
        staged = table[jnp.minimum(slab, table.shape[0] - 1), :, pl.ds(lane, BS)]
        beyond = last[jnp.maximum(slab - table.shape[0], 0), :, pl.ds(lane, BS)]
        parts.append(jnp.where(slab >= table.shape[0], beyond, staged))
    return jnp.concatenate(parts, axis=1)


def slot_product(rows, squares):
    return lax.dot_general(rows, jnp.concatenate(squares, axis=1), NT, preferred_element_type=F32)


def stage_kernel(blocks_ref, *refs):
    parts, (table_ref, squares_ref, sems) = refs[:STAGED], refs[STAGED:]
    size = parts[0].shape[0]
    copies = [pltpu.make_async_copy(blocks_ref.at[k], squares_ref.at[k], sems.at[k]) for k in range(STEPS)]
    for i, part in enumerate(parts):
        copies.append(pltpu.make_async_copy(part, table_ref.at[pl.ds(i * size, size)], sems.at[STEPS + i]))
    for copy in copies:
        copy.start()
    for copy in copies:
        copy.wait()


def field_kernel(now_idx, past_idx, is_last, squares, next_ref, table, last_ref, out_ref, acc):
    for row in range(ROWS):
        last = picked_rows(table, last_ref, past_idx, row * SLOTS)
        at = (row % 2) * SLOTS
        matrix = [next_ref[row // 2, (at + s) * BS : (at + s + 1) * BS] for s in range(SLOTS)]
        acc[row, CH:] = jnp.where(is_last[0] == 1, 0.0, slot_product(last, matrix))
    for k in range(STEPS):
        for row in range(ROWS):
            base = (k * ROWS + row) * SLOTS
            matrix = [squares[k, row, s] for s in range(SLOTS)]
            now = picked_rows(table, last_ref, now_idx, base)
            if k == 0:
                acc[row, :CH] = slot_product(now, matrix)
            else:
                past = picked_rows(table, last_ref, past_idx, base)
                acc[row] += slot_product(jnp.concatenate([now, past]), matrix)
    for row in range(ROWS):
        for f in range(2):
            for z in range(Z):
                start = f * CH + z * CHZ
                out_ref[z, row // 2, row % 2, f] = acc[row, start : start + CHZ]


IN_SMEM = pl.BlockSpec(memory_space=pltpu.SMEM)
IN_VMEM = pl.BlockSpec(memory_space=pltpu.VMEM)
IN_HBM = pl.BlockSpec(memory_space=pltpu.HBM)
ANYWHERE = pl.BlockSpec(memory_space=pl.ANY)
SLAB = (CH, ROWS * BS)
STAGED = 7


def staged(blocks, parts):
    return pl.pallas_call(
        stage_kernel,
        in_specs=[IN_HBM] + [ANYWHERE] * STAGED,
        out_specs=[IN_VMEM] * 2,
        out_shape=[
            jax.ShapeDtypeStruct((STAGED * parts[0].shape[0], *SLAB), BF16),
            jax.ShapeDtypeStruct(blocks.shape, BF16),
        ],
        scratch_shapes=[pltpu.SemaphoreType.DMA((STEPS + STAGED,))],
        compiler_params=pltpu.CompilerParams(vmem_limit_bytes=VMEM_LIMIT),
        cost_estimate=pl.CostEstimate(flops=0, bytes_accessed=1 << 24, transcendentals=0),
        name="staged",
    )(blocks, *parts)


def field_partials(squares, following, table, last, now_idx, past_idx, is_last):
    return pl.pallas_call(
        field_kernel,
        in_specs=[IN_SMEM] * 3 + [IN_VMEM] * 4,
        out_specs=IN_VMEM,
        out_shape=jax.ShapeDtypeStruct((Z, C, 2, 2, CHZ, BS), F32),
        scratch_shapes=[pltpu.VMEM((ROWS, 2 * CH, BS), F32)],
        compiler_params=pltpu.CompilerParams(vmem_limit_bytes=VMEM_LIMIT),
        cost_estimate=pl.CostEstimate(flops=1 << 30, bytes_accessed=1 << 24, transcendentals=0),
        name="field_partials",
    )(now_idx, past_idx, is_last, squares, following, table, last)


def exact_dot(a, b):
    return lax.dot_general(a, b, NT, precision=lax.Precision.HIGHEST, preferred_element_type=F32)


def first_kernel(parts_ref, excite_ref, near_ref, current_ref, low_ref, rest_ref):
    total = parts_ref[0]
    for band in range(1, Z * C):
        total = total + parts_ref[band]
    solved = []
    for row in range(2):
        at = row * 2 * CHZ
        field = excite_ref[0, row] - total[at : at + CHZ]
        solved.append(exact_dot(field, near_ref[row]))
        rest_ref[row] = excite_ref[1, row] - total[at + CHZ : at + 2 * CHZ]
    both = jnp.concatenate(solved, axis=0)
    current_ref[...] = both
    low = both.astype(BF16)
    for s in range(Y * X):
        low_ref[s] = low


def first_solve(parts, excite, near):
    return pl.pallas_call(
        first_kernel,
        out_shape=(
            jax.ShapeDtypeStruct((2 * CHZ, BS), F32),
            jax.ShapeDtypeStruct((Y * X, 2 * CHZ, BS), BF16),
            jax.ShapeDtypeStruct((2, CHZ, BS), F32),
        ),
        compiler_params=pltpu.CompilerParams(vmem_limit_bytes=SMALL_LIMIT),
        name="first_solve",
    )(parts, excite, near)


def second_kernel(idx, mine_ref, other_ref, blocks_ref, rest_ref, near_ref, current_ref, out_ref, table):
    for h, ref in enumerate((mine_ref, other_ref)):
        for s in range(Y * X):
            wide = ref[s].astype(F32)
            for row in range(2):
                table[(h * Y * X + s) * 2 + row] = wide[row * CHZ : (row + 1) * CHZ]
    solved = []
    for row in range(2):
        picked = [table[idx[row * SLOTS + s]].astype(BF16) for s in range(SLOTS)]
        matrix = jnp.concatenate([blocks_ref[(row * SLOTS + s) * BS : (row * SLOTS + s + 1) * BS] for s in range(SLOTS)], axis=1)
        term = lax.dot_general(jnp.concatenate(picked, axis=1), matrix, NT, preferred_element_type=F32)
        solved.append(exact_dot(rest_ref[row] - term, near_ref[row]))
    second = jnp.concatenate(solved, axis=0)
    first = current_ref[...]
    for z in range(Z):
        out_ref[z, 0] = first
        out_ref[z, 1] = second


def second_solve(idx, mine, other, blocks, rest, near, current):
    return pl.pallas_call(
        second_kernel,
        in_specs=[pl.BlockSpec(memory_space=pltpu.SMEM)] + [pl.BlockSpec(memory_space=pltpu.VMEM)] * 6,
        out_specs=pl.BlockSpec(memory_space=pltpu.VMEM),
        out_shape=jax.ShapeDtypeStruct((Z, 2, 2 * CHZ, BS), F32),
        scratch_shapes=[pltpu.VMEM((2 * Y * X * 2, CHZ, BS), F32)],
        compiler_params=pltpu.CompilerParams(vmem_limit_bytes=SMALL_LIMIT),
        name="second_solve",
    )(idx, mine, other, blocks, rest, near, current)


SPREAD = (((0, 2), (7, 5)), ((0, 1), (2, 3), (5, 4), (7, 6)))


def spread(array, step, tie):
    z = lax.axis_index("z")
    received = lax.ppermute(tie(array), "z", SPREAD[step])
    hit = z == SPREAD[step][0][1]
    for _, target in SPREAD[step][1:]:
        hit = hit | (z == target)
    return jnp.where(hit, received, array)


def after(array, *events):
    return lax.optimization_barrier((array, *events))[0]


def local(excitation, history, blocks, pattern, near_inverse):
    core, z = lax.axis_index("core"), lax.axis_index("z")
    bands = lax.axis_size(("z", "core"))

    line = first_axis(history)
    pack = packed_front(blocks, pattern)
    below = hop(line[0], 1, 1)
    above = hop(line[1], 1, -1)
    below_rest = hop(line[1], 1, 1)
    above_rest = hop(after(line[0], below), 1, -1)
    far = hop(below, 1, 1), hop(above, 1, -1)
    following = lax.ppermute(pack, ("z", "core"), [(i, (i - 1) % bands) for i in range(bands)])
    given = jnp.where(core == 0, pack[1], following[0])
    front = jnp.where(z == 0, pack[0], following[1])
    front = jnp.where(core == (z == 0), swap_cores(given), front)
    front = spread(front, 0, lambda new: after(new, below_rest, above_rest))

    pattern = after(pattern, line)
    steps = jnp.arange(STEPS, dtype=jnp.int32)[:, None, None]
    now_idx = entries(pattern, steps)
    past_cols = jnp.concatenate([packed_codes(following[0])[None], pattern[1:]])
    past_idx = entries(past_cols, (steps - 1) % STEPS)
    is_last = (z * C + core == bands - 1).astype(jnp.int32).reshape(1)
    table, squares = staged(blocks, (*line, below, below_rest, above_rest, above, far[0]))
    partial = field_partials(squares, following, table, far[1], now_idx.reshape(-1), past_idx.reshape(-1), is_last)
    parts = lax.all_to_all(partial.reshape(Z * C, 4 * CHZ, BS), ("z", "core"), 0, 0)

    excite = lax.dynamic_slice(excitation, (0, z * CHZ, core * 2 * BS), (2, CHZ, 2 * BS))
    excite = excite.reshape(2, CHZ, 2, BS).transpose(0, 2, 1, 3)
    near = lax.dynamic_slice(near_inverse, (core * 2, 0, 0), (2, BS, BS))
    current, low, rest = first_solve(parts, excite, near)
    front = spread(front, 1, lambda new: new)

    mine = lax.all_to_all(low, ("y", "x"), 0, 0)
    other = swap_cores(mine)
    front_cols = lax.dynamic_slice_in_dim(packed_codes(front), core * 2, 2).reshape(-1)
    front_idx = (((front_cols % ROWS) // 2 ^ core) * Y * X + front_cols // ROWS) * 2 + front_cols % 2
    ready = second_solve(front_idx, mine, other, front, rest, near, current)

    kept = lax.all_to_all(ready, "z", 0, 0)
    given = swap_cores(kept)
    both = jnp.stack([jnp.where(core == 0, kept, given), jnp.where(core == 0, given, kept)])
    both = both.reshape(C, Z, 2, 2, CHZ, BS)
    return both.transpose(2, 1, 4, 0, 3, 5).reshape(2, CH, ROWS * BS)


def solution(mesh):
    split = Mesh(mesh.devices.reshape(Y, X, Z, C), ("y", "x", "z", "core"))
    surf, hist = ("y", "x"), ("z", "core")
    in_specs = (
        P(None, None, surf),
        P(hist, None, surf),
        P(hist, surf, None, None, None),
        P(hist, surf, None),
        P(surf, None, None),
    )
    out_specs = P(None, None, surf)
    return jax.shard_map(local, mesh=split, in_specs=in_specs, out_specs=out_specs, check_vma=False)
```

```python
import jax
import jax.numpy as jnp
from jax import lax
from jax.experimental import pallas as pl
from jax.experimental.pallas import tpu as pltpu
from jax.sharding import Mesh
from jax.sharding import PartitionSpec as P

F32 = jnp.float32
BF16 = jnp.bfloat16
Y, X, Z, C = 4, 4, 8, 2
STEPS, ROWS, SLOTS, BS = 8, 4, 8, 128
CH = 64
CHZ = CH // Z
SIDE = 2 * SLOTS * BS
PAIR = SIDE + 16
NT = (((1,), (1,)), ((), ()))
VMEM_LIMIT = 22 * 1024 * 1024
PACK_LIMIT = 58 * 1024 * 1024
SMALL_LIMIT = 4 * 1024 * 1024


def swap_cores(array):
    return lax.ppermute(array, "core", [(0, 1), (1, 0)])


def hop_pairs(phase, by):
    pairs = []
    for y in range(Y):
        for x in range(X):
            for z in range(Z):
                for core in range(C):
                    if core == phase:
                        to = (y, (x + by) % X)
                    else:
                        to = ((y + by) % Y, x)
                    pairs.append((((y * X + x) * Z + z) * C + core, ((to[0] * X + to[1]) * Z + z) * C + core))
    return pairs


def hop(array, phase, by):
    return lax.ppermute(array, ("y", "x", "z", "core"), hop_pairs(phase, by))


def near_hops(array, phase):
    return hop(array, phase, 1), hop(array, phase, -1)


def first_axis(history):
    below, above = near_hops(history, 0)
    half = STEPS // 2
    far = hop(below[:half], 0, 1), hop(above[half:], 0, -1)
    return jnp.concatenate([history, below]), jnp.concatenate([above, *far])


def entries(cols, steps):
    dy = (lax.axis_index("y") - cols // (X * ROWS)) % Y
    dx = (lax.axis_index("x") - (cols // ROWS) % X) % X
    dy, dx = dy ^ (dy >> 1), dx ^ (dx >> 1)
    slot = jnp.where(lax.axis_index("core") == 0, dy * X + dx, dx * Y + dy)
    return (slot * STEPS + steps) * ROWS + cols % ROWS


def pack_kernel(blocks_ref, pattern_ref, out_ref, codes, sems):
    copies = []
    for pair in range(2):
        for part in range(4):
            size = SIDE // 4
            source = blocks_ref.at[pl.ds(pair * SIDE + part * size, size)]
            target = out_ref.at[pair, pl.ds(part * size, size)]
            copies.append(pltpu.make_async_copy(source, target, sems.at[len(copies)]))
    for copy in copies:
        copy.start()
    codes[...] = jnp.zeros_like(codes)
    codes[:ROWS, :SLOTS] = pattern_ref[0].astype(F32)
    for pair in range(2):
        out_ref[pair, SIDE:] = codes[...].astype(BF16)
    for copy in copies:
        copy.wait()


def packed_front(blocks, pattern):
    return pl.pallas_call(
        pack_kernel,
        in_specs=[pl.BlockSpec(memory_space=pltpu.HBM), pl.BlockSpec(memory_space=pltpu.VMEM)],
        out_specs=pl.BlockSpec(memory_space=pltpu.VMEM),
        out_shape=jax.ShapeDtypeStruct((2, PAIR, BS), BF16),
        scratch_shapes=[pltpu.VMEM((16, BS), F32), pltpu.SemaphoreType.DMA((8,))],
        compiler_params=pltpu.CompilerParams(vmem_limit_bytes=PACK_LIMIT),
        name="packed_front",
    )(blocks.reshape(-1, BS), pattern)


def packed_codes(pack):
    return pack[SIDE : SIDE + ROWS, :SLOTS].astype(jnp.int32)


def picked_rows(table, last, idx, base):
    parts = []
    for s in range(SLOTS):
        code = idx[base + s]
        lane = pl.multiple_of(lax.rem(code, ROWS) * BS, BS)
        slab = lax.div(code, ROWS)
        staged = table[jnp.minimum(slab, table.shape[0] - 1), :, pl.ds(lane, BS)]
        beyond = last[jnp.maximum(slab - table.shape[0], 0), :, pl.ds(lane, BS)]
        parts.append(lax.select(slab >= table.shape[0], beyond, staged))
    return jnp.concatenate(parts, axis=1)


def slot_product(rows, squares):
    return lax.dot_general(rows, jnp.concatenate(squares, axis=1), NT, preferred_element_type=F32)


def stage_kernel(blocks_ref, *refs):
    parts, (table_ref, squares_ref, sems) = refs[:STAGED], refs[STAGED:]
    size = parts[0].shape[0]
    copies = [pltpu.make_async_copy(blocks_ref.at[k], squares_ref.at[k], sems.at[k]) for k in range(STEPS)]
    for i, part in enumerate(parts):
        copies.append(pltpu.make_async_copy(part, table_ref.at[pl.ds(i * size, size)], sems.at[STEPS + i]))
    for copy in copies:
        copy.start()
    for copy in copies:
        copy.wait()


def field_kernel(now_idx, past_idx, is_last, squares, next_ref, table, last_ref, out_ref, acc):
    for row in range(ROWS):
        last = picked_rows(table, last_ref, past_idx, row * SLOTS)
        at = (row % 2) * SLOTS
        matrix = [next_ref[row // 2, (at + s) * BS : (at + s + 1) * BS] for s in range(SLOTS)]
        acc[row, CH:] = jnp.where(is_last[0] == 1, 0.0, slot_product(last, matrix))
    for k in range(STEPS):
        for row in range(ROWS):
            base = (k * ROWS + row) * SLOTS
            matrix = [squares[k, row, s] for s in range(SLOTS)]
            now = picked_rows(table, last_ref, now_idx, base)
            if k == 0:
                acc[row, :CH] = slot_product(now, matrix)
            else:
                past = picked_rows(table, last_ref, past_idx, base)
                acc[row] += slot_product(jnp.concatenate([now, past]), matrix)
    for row in range(ROWS):
        for f in range(2):
            for z in range(Z):
                start = f * CH + z * CHZ
                out_ref[z, row // 2, row % 2, f] = acc[row, start : start + CHZ]


IN_SMEM = pl.BlockSpec(memory_space=pltpu.SMEM)
IN_VMEM = pl.BlockSpec(memory_space=pltpu.VMEM)
IN_HBM = pl.BlockSpec(memory_space=pltpu.HBM)
ANYWHERE = pl.BlockSpec(memory_space=pl.ANY)
SLAB = (CH, ROWS * BS)
STAGED = 7


def staged(blocks, parts):
    return pl.pallas_call(
        stage_kernel,
        in_specs=[IN_HBM] + [ANYWHERE] * STAGED,
        out_specs=[IN_VMEM] * 2,
        out_shape=[
            jax.ShapeDtypeStruct((STAGED * parts[0].shape[0], *SLAB), BF16),
            jax.ShapeDtypeStruct(blocks.shape, BF16),
        ],
        scratch_shapes=[pltpu.SemaphoreType.DMA((STEPS + STAGED,))],
        compiler_params=pltpu.CompilerParams(vmem_limit_bytes=VMEM_LIMIT),
        cost_estimate=pl.CostEstimate(flops=0, bytes_accessed=1 << 24, transcendentals=0),
        name="staged",
    )(blocks, *parts)


def field_partials(squares, following, table, last, now_idx, past_idx, is_last):
    return pl.pallas_call(
        field_kernel,
        in_specs=[IN_SMEM] * 3 + [IN_VMEM] * 4,
        out_specs=IN_VMEM,
        out_shape=jax.ShapeDtypeStruct((Z, C, 2, 2, CHZ, BS), F32),
        scratch_shapes=[pltpu.VMEM((ROWS, 2 * CH, BS), F32)],
        compiler_params=pltpu.CompilerParams(vmem_limit_bytes=VMEM_LIMIT),
        cost_estimate=pl.CostEstimate(flops=1 << 30, bytes_accessed=1 << 24, transcendentals=0),
        name="field_partials",
    )(now_idx, past_idx, is_last, squares, following, table, last)


def exact_dot(a, b):
    return lax.dot_general(a, b, NT, precision=lax.Precision.HIGHEST, preferred_element_type=F32)


def first_kernel(parts_ref, excite_ref, near_ref, current_ref, low_ref, rest_ref):
    total = parts_ref[0]
    for band in range(1, Z * C):
        total = total + parts_ref[band]
    solved = []
    for row in range(2):
        at = row * 2 * CHZ
        field = excite_ref[0, row] - total[at : at + CHZ]
        solved.append(exact_dot(field, near_ref[row]))
        rest_ref[row] = excite_ref[1, row] - total[at + CHZ : at + 2 * CHZ]
    both = jnp.concatenate(solved, axis=0)
    current_ref[...] = both
    low = both.astype(BF16)
    for s in range(Y * X):
        low_ref[s] = low


def first_solve(parts, excite, near):
    return pl.pallas_call(
        first_kernel,
        out_shape=(
            jax.ShapeDtypeStruct((2 * CHZ, BS), F32),
            jax.ShapeDtypeStruct((Y * X, 2 * CHZ, BS), BF16),
            jax.ShapeDtypeStruct((2, CHZ, BS), F32),
        ),
        compiler_params=pltpu.CompilerParams(vmem_limit_bytes=SMALL_LIMIT),
        name="first_solve",
    )(parts, excite, near)


def second_kernel(idx, mine_ref, other_ref, blocks_ref, rest_ref, near_ref, current_ref, out_ref, table):
    for h, ref in enumerate((mine_ref, other_ref)):
        for s in range(Y * X):
            wide = ref[s].astype(F32)
            for row in range(2):
                table[(h * Y * X + s) * 2 + row] = wide[row * CHZ : (row + 1) * CHZ]
    solved = []
    for row in range(2):
        picked = [table[idx[row * SLOTS + s]].astype(BF16) for s in range(SLOTS)]
        matrix = jnp.concatenate([blocks_ref[(row * SLOTS + s) * BS : (row * SLOTS + s + 1) * BS] for s in range(SLOTS)], axis=1)
        term = lax.dot_general(jnp.concatenate(picked, axis=1), matrix, NT, preferred_element_type=F32)
        solved.append(exact_dot(rest_ref[row] - term, near_ref[row]))
    second = jnp.concatenate(solved, axis=0)
    first = current_ref[...]
    for z in range(Z):
        out_ref[z, 0] = first
        out_ref[z, 1] = second


def second_solve(idx, mine, other, blocks, rest, near, current):
    return pl.pallas_call(
        second_kernel,
        in_specs=[pl.BlockSpec(memory_space=pltpu.SMEM)] + [pl.BlockSpec(memory_space=pltpu.VMEM)] * 6,
        out_specs=pl.BlockSpec(memory_space=pltpu.VMEM),
        out_shape=jax.ShapeDtypeStruct((Z, 2, 2 * CHZ, BS), F32),
        scratch_shapes=[pltpu.VMEM((2 * Y * X * 2, CHZ, BS), F32)],
        compiler_params=pltpu.CompilerParams(vmem_limit_bytes=SMALL_LIMIT),
        name="second_solve",
    )(idx, mine, other, blocks, rest, near, current)


SPREAD = (((0, 2), (7, 5)), ((0, 1), (2, 3), (5, 4), (7, 6)))


def spread(array, step, tie):
    z = lax.axis_index("z")
    received = lax.ppermute(tie(array), "z", SPREAD[step])
    hit = z == SPREAD[step][0][1]
    for _, target in SPREAD[step][1:]:
        hit = hit | (z == target)
    return jnp.where(hit, received, array)


def after(array, *events):
    return lax.optimization_barrier((array, *events))[0]


def local(excitation, history, blocks, pattern, near_inverse):
    core, z = lax.axis_index("core"), lax.axis_index("z")
    bands = lax.axis_size(("z", "core"))

    line = first_axis(history)
    pack = packed_front(blocks, pattern)
    below = hop(line[0], 1, 1)
    above = hop(line[1], 1, -1)
    below_rest = hop(line[1], 1, 1)
    above_rest = hop(after(line[0], below), 1, -1)
    far = hop(below, 1, 1), hop(above, 1, -1)
    following = lax.ppermute(pack, ("z", "core"), [(i, (i - 1) % bands) for i in range(bands)])
    given = jnp.where(core == 0, pack[1], following[0])
    front = jnp.where(z == 0, pack[0], following[1])
    front = jnp.where(core == (z == 0), swap_cores(given), front)
    front = spread(front, 0, lambda new: after(new, below_rest, above_rest))

    pattern = after(pattern, line)
    steps = jnp.arange(STEPS, dtype=jnp.int32)[:, None, None]
    now_idx = entries(pattern, steps)
    past_cols = jnp.concatenate([packed_codes(following[0])[None], pattern[1:]])
    past_idx = entries(past_cols, (steps - 1) % STEPS)
    is_last = (z * C + core == bands - 1).astype(jnp.int32).reshape(1)
    table, squares = staged(blocks, (*line, below, below_rest, above_rest, above, far[0]))
    partial = field_partials(squares, following, table, far[1], now_idx.reshape(-1), past_idx.reshape(-1), is_last)
    parts = lax.all_to_all(partial.reshape(Z * C, 4 * CHZ, BS), ("z", "core"), 0, 0)

    excite = lax.dynamic_slice(excitation, (0, z * CHZ, core * 2 * BS), (2, CHZ, 2 * BS))
    excite = excite.reshape(2, CHZ, 2, BS).transpose(0, 2, 1, 3)
    near = lax.dynamic_slice(near_inverse, (core * 2, 0, 0), (2, BS, BS))
    current, low, rest = first_solve(parts, excite, near)
    front = spread(front, 1, lambda new: new)

    mine = lax.all_to_all(low, ("y", "x"), 0, 0)
    other = swap_cores(mine)
    front_cols = lax.dynamic_slice_in_dim(packed_codes(front), core * 2, 2).reshape(-1)
    front_idx = (((front_cols % ROWS) // 2 ^ core) * Y * X + front_cols // ROWS) * 2 + front_cols % 2
    ready = second_solve(front_idx, mine, other, front, rest, near, current)

    kept = lax.all_to_all(ready, "z", 0, 0)
    given = swap_cores(kept)
    both = jnp.stack([jnp.where(core == 0, kept, given), jnp.where(core == 0, given, kept)])
    both = both.reshape(C, Z, 2, 2, CHZ, BS)
    return both.transpose(2, 1, 4, 0, 3, 5).reshape(2, CH, ROWS * BS)


def solution(mesh):
    split = Mesh(mesh.devices.reshape(Y, X, Z, C), ("y", "x", "z", "core"))
    surf, hist = ("y", "x"), ("z", "core")
    in_specs = (
        P(None, None, surf),
        P(hist, None, surf),
        P(hist, surf, None, None, None),
        P(hist, surf, None),
        P(surf, None, None),
    )
    out_specs = P(None, None, surf)
    return jax.shard_map(local, mesh=split, in_specs=in_specs, out_specs=out_specs, check_vma=False)
```
